32 devices in a mesh: rep: 4 (over y, x), fsdp: 8 (over z, core).
Axes of the slice: x: 2, y: 2, z: 4, core: 2. Of those that a mesh axis runs over, the one named last changes fastest.
Arguments:
- tokens: bfloat16 [49152, 576], P(('rep', 'fsdp')), may hold values from -6 to 6
- segment: int32 [49152], P(('rep', 'fsdp')), may hold values from -1 to 767, as said below
- attn_gain: bfloat16 [2, 576], P(None, 'fsdp'), may hold values from 0.099609375 to 1.8984375
- w_query: bfloat16 [2, 576, 576], P(None, 'fsdp'), may hold values from -0.25 to 0.25
- key_weight: bfloat16 [2, 576, 192], P(None, 'fsdp'), may hold values from -0.25 to 0.25
- value_weight: bfloat16 [2, 576, 192], P(None, 'fsdp'), may hold values from -0.25 to 0.25
- w_out: bfloat16 [2, 576, 576], P(None, 'fsdp'), may hold values from -3 to 3
- mlp_gain: bfloat16 [2, 576], P(None, 'fsdp'), may hold values from 0.099609375 to 1.8984375
- gate_weight: bfloat16 [2, 576, 1536], P(None, 'fsdp'), may hold values from -0.25 to 0.25
- up_weight: bfloat16 [2, 576, 1536], P(None, 'fsdp'), may hold values from -0.25 to 0.25
- down_weight: bfloat16 [2, 1536, 576], P(None, 'fsdp'), may hold values from -0.15625 to 0.15625
- cotangent: bfloat16 [49152, 576], P(('rep', 'fsdp')), may hold values from -6 to 6
Outputs:
- out_tokens: bfloat16 [49152, 576], P(('rep', 'fsdp'))
- grad_tokens: float32 [49152, 576], P(('rep', 'fsdp'))
- grad_attn_gain: float32 [2, 576], P(None, 'fsdp')
- grad_query: float32 [2, 576, 576], P(None, 'fsdp')
- grad_key: float32 [2, 576, 192], P(None, 'fsdp')
- grad_value: float32 [2, 576, 192], P(None, 'fsdp')
- grad_out: float32 [2, 576, 576], P(None, 'fsdp')
- grad_mlp_gain: float32 [2, 576], P(None, 'fsdp')
- grad_gate: float32 [2, 576, 1536], P(None, 'fsdp')
- grad_up: float32 [2, 576, 1536], P(None, 'fsdp')
- grad_down: float32 [2, 1536, 576], P(None, 'fsdp')
The draws below stay inside these ranges and needn't reach their ends.
Inputs may be any that keep to these rules, and one draw needn't show every extreme that they name: `segment`: each aligned block of 768 rows (one micro-batch of one device) holds whole sequences numbered 0, 1, 2, ... in order, then padding rows marked -1; no sequence has more than 512 rows and one has exactly 512; some block has no padding; some block holds 768 sequences of one row each.
All inputs are finite; a program needn't handle non-finite values.
Results may differ from the reference program's by a relative error of at most 0.025.
Values may be sent and summed in bfloat16 or wider, within the bound.
A program may use at most 384 MiB of HBM per device.

```python
import jax
import jax.numpy as jnp
from jax import lax

MODEL_WIDTH = 576
QUERY_HEADS = 9
KEY_VALUE_HEADS = 3
HEAD_WIDTH = 64
FF = 1536
DECODER_LAYERS = 2
MICRO = 2
SEQ_MAX = 512
MB_ROWS = 768
TOK_DEV = 1536
TOKENS = 49152


def draw_segment(key, part):
    blocks = TOKENS // MB_ROWS
    subkeys = jax.random.split(key, 3)
    row_index = jnp.arange(MB_ROWS, dtype=jnp.int32)
    block_index = jnp.arange(blocks, dtype=jnp.int32)[:, None]
    boundary = jax.random.randint(subkeys[0], (blocks, MB_ROWS), 0, SEQ_MAX) < 3
    full_block = jax.random.randint(subkeys[1], (), 0, blocks)
    single_block = (full_block + 1) % blocks
    full_rows = block_index == full_block
    single_rows = block_index == single_block
    boundary = jnp.where(full_rows & (row_index[None, :] < SEQ_MAX), False, boundary)
    boundary = boundary | (row_index % SEQ_MAX == 0)[None, :]
    boundary = boundary | single_rows
    live_count = jax.random.randint(subkeys[2], (blocks, 1), MB_ROWS // 4, MB_ROWS + 1)
    live_count = jnp.where(full_rows | single_rows, MB_ROWS, live_count)
    numbers = jnp.cumsum(boundary.astype(jnp.int32), axis=1) - 1
    numbers = jnp.where(row_index[None, :] < live_count, numbers, -1)
    return numbers.reshape(TOKENS).astype(jnp.int32)


def block_levels(rng, dims, shards, smallest, high):
    level = 1.0
    for dim, parts in shards:
        draws = jax.random.uniform(jax.random.fold_in(jax.random.fold_in(rng, 6), dim), (parts,), jnp.float32, smallest / len(shards), high / len(shards))
        level = level * jnp.repeat(jnp.exp(draws), dims[dim] // parts).reshape((-1,) + (1,) * (len(dims) - 1 - dim))
    return level


def scatter_about(stream_key, extent, scale, bound, pieces=(), held_as=jnp.bfloat16):
    entries = jax.random.normal(stream_key, extent, jnp.float32) * scale
    if len(pieces) > 0:
        entries = block_levels(stream_key, extent, pieces, -0.22, 0.18) * entries
    return jnp.clip(entries, min=-bound, max=bound).astype(held_as)


def setup_inputs(seed: int = 0) -> dict:
    key_of = jax.random.split(jax.random.key(seed), 13)
    return {
        "tokens": scatter_about(key_of[0], (TOKENS, MODEL_WIDTH), 1.0, 6.0, ((0, 32),)),
        "segment": draw_segment(jax.random.fold_in(key_of[12], 71), 0),
        "attn_gain": jnp.clip(1.0 + 0.18 * jax.random.normal(key_of[2], (DECODER_LAYERS, MODEL_WIDTH), jnp.float32), 0.099609375, 1.8984375).astype(jnp.bfloat16),
        "w_query": scatter_about(key_of[3], (DECODER_LAYERS, MODEL_WIDTH, QUERY_HEADS * HEAD_WIDTH), MODEL_WIDTH ** -0.5, 0.25, ((1, 8),)),
        "key_weight": scatter_about(key_of[4], (DECODER_LAYERS, MODEL_WIDTH, KEY_VALUE_HEADS * HEAD_WIDTH), MODEL_WIDTH ** -0.5, 0.25, ((1, 8),)),
        "value_weight": scatter_about(key_of[5], (DECODER_LAYERS, MODEL_WIDTH, KEY_VALUE_HEADS * HEAD_WIDTH), MODEL_WIDTH ** -0.5, 0.25, ((1, 8),)),
        "w_out": scatter_about(key_of[6], (DECODER_LAYERS, QUERY_HEADS * HEAD_WIDTH, MODEL_WIDTH), (max(QUERY_HEADS * HEAD_WIDTH * 4 // SEQ_MAX, 4)) ** -0.5, 3.0, ((1, 8),)),
        "mlp_gain": jnp.clip(1.0 + 0.18 * jax.random.normal(key_of[7], (DECODER_LAYERS, MODEL_WIDTH), jnp.float32), 0.099609375, 1.8984375).astype(jnp.bfloat16),
        "gate_weight": scatter_about(key_of[8], (DECODER_LAYERS, MODEL_WIDTH, FF), MODEL_WIDTH ** -0.5, 0.25, ((1, 8),)),
        "up_weight": scatter_about(key_of[9], (DECODER_LAYERS, MODEL_WIDTH, FF), MODEL_WIDTH ** -0.5, 0.25, ((1, 8),)),
        "down_weight": scatter_about(key_of[10], (DECODER_LAYERS, FF, MODEL_WIDTH), FF ** -0.5, 0.15625, ((1, 8),)),
        "cotangent": scatter_about(key_of[11], (TOKENS, MODEL_WIDTH), 1.0, 6.0, ((0, 32),)),
    }


@jax.custom_vjp
def lower_precision(v):
    return lax.optimization_barrier(v.astype(jnp.bfloat16)).astype(jnp.float32)

@jax.custom_vjp
def lower_precision_back(v):
    return v

def low_keep(v):
    return (lower_precision(v), None)

def low_pass(kept, grad):
    return (grad,)

def back_keep(v):
    return (v, None)

def back_low(kept, grad):
    return (lower_precision(grad),)
lower_precision.defvjp(low_keep, low_pass)
lower_precision_back.defvjp(back_keep, back_low)
epsilon = 1e-05
rope_base = 100000.0
masked_fill = -1e+30
highest_precision = lax.Precision.HIGHEST

def geometry(segment):
    count_of_rows = segment.shape[-1]
    row_index = jnp.arange(count_of_rows, dtype=jnp.int32)
    same_segment = segment[..., :, None] == segment[..., None, :]
    earlier = row_index[None, :] < row_index[:, None]
    position = lax.optimization_barrier(jnp.sum(jnp.where(same_segment & earlier, 1, 0).astype(jnp.int32), axis=-1))
    allowed = same_segment & (row_index[None, :] <= row_index[:, None])
    active_rows = jnp.where(segment >= 0, 1.0, 0.0).astype(jnp.float32)[..., None]
    frequency = rope_base ** (-2.0 * jnp.arange(HEAD_WIDTH // 2, dtype=jnp.float32) / HEAD_WIDTH)
    angles = position.astype(jnp.float32)[..., None] * frequency
    return (allowed, active_rows, jnp.cos(angles)[..., None, :], jnp.sin(angles)[..., None, :])

def rotary_apply(vectors, cosine_table, sine_values):
    half_width = vectors.shape[-1] // 2
    first_half = vectors[..., :half_width]
    second_half = vectors[..., half_width:]
    return jnp.concatenate([first_half * cosine_table - second_half * sine_values, second_half * cosine_table + first_half * sine_values], axis=-1)

def norm_apply(value_rows, gain_row):
    factor = lax.rsqrt(lax.optimization_barrier(jnp.mean(value_rows * value_rows, axis=-1, keepdims=True)) + epsilon)
    return value_rows * factor * gain_row

def layer_apply(residual, params, layout):
    attn_gain, w_query, key_weight, value_weight, w_out, mlp_gain, gate_weight, up_weight, down_weight = params
    allowed, active_rows, cosine_table, sine_values = layout
    leading_block = residual.shape[:-1]
    scale = HEAD_WIDTH ** (-0.5)
    normed = lower_precision(norm_apply(residual, attn_gain))
    query_rows = lower_precision_back(jnp.einsum('mrd,de->mre', normed, w_query, precision=highest_precision))
    key_rows = lower_precision_back(jnp.einsum('mrd,de->mre', normed, key_weight, precision=highest_precision))
    value_rows = lower_precision_back(jnp.einsum('mrd,de->mre', normed, value_weight, precision=highest_precision))
    query_rows = lower_precision(rotary_apply(query_rows.reshape(leading_block + (QUERY_HEADS, HEAD_WIDTH)), cosine_table, sine_values))
    key_rows = lower_precision(rotary_apply(key_rows.reshape(leading_block + (KEY_VALUE_HEADS, HEAD_WIDTH)), cosine_table, sine_values))
    value_rows = lower_precision(value_rows).reshape(leading_block + (KEY_VALUE_HEADS, HEAD_WIDTH))
    grouped_heads = query_rows.reshape(leading_block + (KEY_VALUE_HEADS, QUERY_HEADS // KEY_VALUE_HEADS, HEAD_WIDTH))
    scores = lower_precision_back(jnp.einsum('mqgjd,mkgd->mgjqk', grouped_heads, key_rows, precision=highest_precision) * scale)
    masked = jnp.where(allowed[:, None, None], scores, masked_fill)
    probs = lower_precision(jax.nn.softmax(masked, axis=-1))
    mixed = jnp.einsum('mgjqk,mkgd->mqgjd', probs, value_rows, precision=highest_precision).reshape(leading_block + (QUERY_HEADS * HEAD_WIDTH,))
    mixed = lower_precision(lower_precision_back(mixed))
    hidden_state = residual + lower_precision_back(jnp.einsum('mre,ed->mrd', mixed, w_out, precision=highest_precision)) * active_rows
    normed_feed_input = lower_precision(norm_apply(hidden_state, mlp_gain))
    gate_branch = lower_precision_back(jnp.einsum('hwl,la->hwa', normed_feed_input, gate_weight, precision=highest_precision))
    up_branch = lower_precision_back(jnp.einsum('hwl,la->hwa', normed_feed_input, up_weight, precision=highest_precision))
    inner_product = lower_precision(lower_precision_back(jax.nn.silu(gate_branch) * up_branch))
    return hidden_state + lower_precision_back(jnp.einsum('ews,sn->ewn', inner_product, down_weight, precision=highest_precision)) * active_rows

def reference(tokens, segment, attn_gain, w_query, key_weight, value_weight, w_out, mlp_gain, gate_weight, up_weight, down_weight, cotangent):
    groups = TOKENS // TOK_DEV
    weights = tuple((item.astype(jnp.float32) for item in (attn_gain, w_query, key_weight, value_weight, w_out, mlp_gain, gate_weight, up_weight, down_weight)))
    seg_groups = segment.reshape(groups, MICRO, MB_ROWS)

    def forward(residual, params):

        def one_group(paired):
            value_rows, seg_rows = paired
            layout = geometry(seg_rows)
            for layer_index in range(DECODER_LAYERS):
                value_rows = layer_apply(value_rows, tuple((weight[layer_index] for weight in params)), layout)
            return value_rows
        result = lax.map(jax.checkpoint(one_group), (residual.reshape(groups, MICRO, MB_ROWS, MODEL_WIDTH), seg_groups))
        return result.reshape(TOKENS, MODEL_WIDTH)
    result, pullback = jax.vjp(forward, tokens.astype(jnp.float32), weights)
    grad_input, grad_params = pullback(cotangent.astype(jnp.float32))
    return (result.astype(jnp.bfloat16), grad_input, grad_params[0], grad_params[1], grad_params[2], grad_params[3], grad_params[4], grad_params[5], grad_params[6], grad_params[7], grad_params[8])
```

```python
import jax
import jax.numpy as jnp
from jax import lax
from jax.sharding import PartitionSpec as P

QUERY_HEADS = 9
KEY_VALUE_HEADS = 3
HEAD_WIDTH = 64
DECODER_LAYERS = 2
MICRO = 2


epsilon = 1e-05
rope_base = 100000.0
masked_fill = -1e30


def geometry(segment):
    count_of_rows = segment.shape[-1]
    row_index = jnp.arange(count_of_rows, dtype=jnp.int32)
    same_segment = segment[..., :, None] == segment[..., None, :]
    earlier = row_index[None, :] < row_index[:, None]
    position = jnp.sum(jnp.where(same_segment & earlier, 1, 0).astype(jnp.int32), axis=-1)
    allowed = same_segment & (row_index[None, :] <= row_index[:, None])
    active_rows = jnp.where(segment >= 0, 1.0, 0.0).astype(jnp.float32)[..., None]
    frequency = rope_base ** (-2.0 * jnp.arange(HEAD_WIDTH // 2, dtype=jnp.float32) / HEAD_WIDTH)
    angles = position.astype(jnp.float32)[..., None] * frequency
    return (allowed, active_rows, jnp.cos(angles)[..., None, :], jnp.sin(angles)[..., None, :])


def rotary_apply(vectors, cosine_table, sine_values):
    half_width = vectors.shape[-1] // 2
    first_half = vectors[..., :half_width]
    second_half = vectors[..., half_width:]
    return jnp.concatenate(
        [
            first_half * cosine_table - second_half * sine_values,
            second_half * cosine_table + first_half * sine_values,
        ],
        axis=-1,
    )


def rotary_inverse(vectors, cosine_table, sine_values):
    half_width = vectors.shape[-1] // 2
    first_half = vectors[..., :half_width]
    second_half = vectors[..., half_width:]
    return jnp.concatenate(
        [
            first_half * cosine_table + second_half * sine_values,
            second_half * cosine_table - first_half * sine_values,
        ],
        axis=-1,
    )


def norm_forward(value_rows, gain_row):
    factor = lax.rsqrt(jnp.mean(value_rows * value_rows, axis=-1, keepdims=True) + epsilon)
    return (value_rows * factor * gain_row, factor)


def norm_backward(value_rows, factor, gain_row, upstream):
    scaled = upstream * gain_row
    through = factor * scaled - value_rows * (factor * factor * factor) * jnp.mean(
        scaled * value_rows, axis=-1, keepdims=True
    )
    return (through, jnp.sum(upstream * value_rows * factor, axis=0))


def attention_forward(query_rows, key_rows, value_rows, allowed):
    count_of_rows = query_rows.shape[0]
    queries = query_rows.reshape(
        count_of_rows, KEY_VALUE_HEADS, QUERY_HEADS // KEY_VALUE_HEADS, HEAD_WIDTH
    )
    keys = key_rows.reshape(count_of_rows, KEY_VALUE_HEADS, HEAD_WIDTH)
    values = value_rows.reshape(count_of_rows, KEY_VALUE_HEADS, HEAD_WIDTH)
    scores = jnp.einsum(
        "qgjd,kgd->gjqk", queries, keys, preferred_element_type=jnp.float32
    ) * HEAD_WIDTH ** (-0.5)
    scores = jnp.where(allowed, scores, masked_fill)
    peak = jnp.max(scores, axis=-1, keepdims=True)
    expo = jnp.exp(scores - peak)
    total = jnp.sum(expo, axis=-1, keepdims=True)
    probs = (expo / total).astype(jnp.bfloat16)
    mixed = jnp.einsum("gjqk,kgd->qgjd", probs, values, preferred_element_type=jnp.float32)
    mixed = mixed.reshape(count_of_rows, QUERY_HEADS * HEAD_WIDTH).astype(jnp.bfloat16)
    return (mixed, peak + jnp.log(total))


def attention_backward(query_rows, key_rows, value_rows, log_total, mixed_gradient, allowed):
    count_of_rows = query_rows.shape[0]
    scale = HEAD_WIDTH ** (-0.5)
    group_shape = (count_of_rows, KEY_VALUE_HEADS, QUERY_HEADS // KEY_VALUE_HEADS, HEAD_WIDTH)
    queries = query_rows.reshape(group_shape)
    keys = key_rows.reshape(count_of_rows, KEY_VALUE_HEADS, HEAD_WIDTH)
    values = value_rows.reshape(count_of_rows, KEY_VALUE_HEADS, HEAD_WIDTH)
    mixed_gradient = mixed_gradient.reshape(group_shape)
    scores = jnp.einsum("qgjd,kgd->gjqk", queries, keys, preferred_element_type=jnp.float32) * scale
    scores = jnp.where(allowed, scores, masked_fill)
    probs_full = jnp.exp(scores - log_total)
    probs = probs_full.astype(jnp.bfloat16)
    value_gradient = jnp.einsum(
        "gjqk,qgjd->kgd", probs, mixed_gradient, preferred_element_type=jnp.float32
    )
    grad_probs = jnp.einsum(
        "qgjd,kgd->gjqk", mixed_gradient, values, preferred_element_type=jnp.float32
    )
    row_weight = jnp.sum(probs_full * grad_probs, axis=-1, keepdims=True)
    grad_scores = (probs_full * (grad_probs - row_weight)).astype(jnp.bfloat16)
    grad_queries = (
        jnp.einsum("gjqk,kgd->qgjd", grad_scores, keys, preferred_element_type=jnp.float32) * scale
    )
    key_gradient = (
        jnp.einsum("gjqk,qgjd->kgd", grad_scores, queries, preferred_element_type=jnp.float32)
        * scale
    )
    return (
        grad_queries.reshape(count_of_rows, -1),
        key_gradient.reshape(count_of_rows, -1),
        value_gradient.reshape(count_of_rows, -1),
    )


def rotate_flat(rotation, rows, cosine_table, sine_values):
    shaped = rows.reshape(rows.shape[0], -1, HEAD_WIDTH)
    return rotation(shaped, cosine_table, sine_values).reshape(rows.shape).astype(jnp.bfloat16)


def layer_forward(residual, attn_params, fetch_feed, gains, layout):
    allowed, active_rows, cosine_table, sine_values = layout
    w_query, key_weight, value_weight, w_out = attn_params
    normed, factor = norm_forward(residual, gains[0])
    normed = normed.astype(jnp.bfloat16)
    query_rows = jnp.dot(normed, w_query, preferred_element_type=jnp.float32)
    key_rows = jnp.dot(normed, key_weight, preferred_element_type=jnp.float32)
    value_rows = jnp.dot(normed, value_weight, preferred_element_type=jnp.float32).astype(
        jnp.bfloat16
    )
    query_rows = rotate_flat(rotary_apply, query_rows, cosine_table, sine_values)
    key_rows = rotate_flat(rotary_apply, key_rows, cosine_table, sine_values)
    mixed, log_total = attend(query_rows, key_rows, value_rows, allowed)
    hidden_state = (
        residual + jnp.dot(mixed, w_out, preferred_element_type=jnp.float32) * active_rows
    )
    gate_weight, up_weight, down_weight = fetch_feed
    normed_feed, factor_mlp = norm_forward(hidden_state, gains[1])
    normed_feed = normed_feed.astype(jnp.bfloat16)
    gate_branch = jnp.dot(normed_feed, gate_weight, preferred_element_type=jnp.float32)
    up_branch = jnp.dot(normed_feed, up_weight, preferred_element_type=jnp.float32)
    inner_product = (jax.nn.silu(gate_branch) * up_branch).astype(jnp.bfloat16)
    output = (
        hidden_state
        + jnp.dot(inner_product, down_weight, preferred_element_type=jnp.float32) * active_rows
    )
    saved = (
        residual,
        normed,
        factor,
        query_rows,
        key_rows,
        value_rows,
        mixed,
        log_total,
        hidden_state,
        normed_feed,
        factor_mlp,
        gate_branch,
        up_branch,
        inner_product,
    )
    return (output, saved)


def contract_rows(left, right):
    return lax.dot_general(
        left, right, (((0,), (0,)), ((), ())), preferred_element_type=jnp.float32
    ).astype(jnp.bfloat16)


def times_transposed(left, right):
    return lax.dot_general(
        left, right, (((1,), (1,)), ((), ())), preferred_element_type=jnp.float32
    )


def feed_backward(saved, feed_params, gain_row, active_rows, upstream):
    hidden_state, normed_feed, factor_mlp, gate_branch, up_branch, inner_product = saved[8:]
    gate_weight, up_weight, down_weight = feed_params
    sigmoid_gate = jax.nn.sigmoid(gate_branch)
    activated = gate_branch * sigmoid_gate
    grad_branch = (upstream * active_rows).astype(jnp.bfloat16)
    grad_inner = times_transposed(grad_branch, down_weight).astype(jnp.bfloat16)
    grad_gate_in = (
        grad_inner * up_branch * sigmoid_gate * (1.0 + gate_branch * (1.0 - sigmoid_gate))
    ).astype(jnp.bfloat16)
    grad_up_in = (grad_inner * activated).astype(jnp.bfloat16)
    grad_down = contract_rows(inner_product, grad_branch)
    grad_gate = contract_rows(normed_feed, grad_gate_in)
    grad_up = contract_rows(normed_feed, grad_up_in)
    grad_normed = times_transposed(grad_gate_in, gate_weight) + times_transposed(
        grad_up_in, up_weight
    )
    through, grad_gain = norm_backward(hidden_state, factor_mlp, gain_row, grad_normed)
    return (through + upstream, grad_gain, (grad_gate, grad_up, grad_down))


def attention_part_backward(saved, attn_params, gain_row, layout, grad_hidden):
    residual, normed, factor, query_rows, key_rows, value_rows, mixed, log_total = saved[:8]
    w_query, key_weight, value_weight, w_out = attn_params
    allowed, active_rows, cosine_table, sine_values = layout
    grad_attn = (grad_hidden * active_rows).astype(jnp.bfloat16)
    grad_out = contract_rows(mixed, grad_attn)
    mixed_gradient = times_transposed(grad_attn, w_out).astype(jnp.bfloat16)
    grad_queries, key_gradient, value_gradient = attend_back(
        query_rows, key_rows, value_rows, log_total, mixed_gradient, allowed
    )
    value_gradient = value_gradient.astype(jnp.bfloat16)
    grad_queries = rotate_flat(rotary_inverse, grad_queries, cosine_table, sine_values)
    key_gradient = rotate_flat(rotary_inverse, key_gradient, cosine_table, sine_values)
    grad_query = contract_rows(normed, grad_queries)
    grad_key = contract_rows(normed, key_gradient)
    grad_value = contract_rows(normed, value_gradient)
    grad_normed = (
        times_transposed(grad_queries, w_query)
        + times_transposed(key_gradient, key_weight)
        + times_transposed(value_gradient, value_weight)
    )
    through, grad_gain = norm_backward(residual, factor, gain_row, grad_normed)
    return (through + grad_hidden, grad_gain, (grad_query, grad_key, grad_value, grad_out))


def blocks_of(rows):
    size = rows.shape[0] // MICRO
    return [rows[index * size : (index + 1) * size] for index in range(MICRO)]


def attend(query_rows, key_rows, value_rows, allowed):
    results = [
        attention_forward(*piece)
        for piece in zip(blocks_of(query_rows), blocks_of(key_rows), blocks_of(value_rows), allowed)
    ]
    return (jnp.concatenate([item[0] for item in results]), [item[1] for item in results])


def attend_back(query_rows, key_rows, value_rows, log_total, mixed_gradient, allowed):
    results = [
        attention_backward(*piece)
        for piece in zip(
            blocks_of(query_rows),
            blocks_of(key_rows),
            blocks_of(value_rows),
            log_total,
            blocks_of(mixed_gradient),
            allowed,
        )
    ]
    return tuple(jnp.concatenate([item[member] for item in results]) for member in range(3))


def sum_shards(buffer, last):
    shard = lax.psum_scatter(buffer, "fsdp", scatter_dimension=0, tiled=False)
    if last:
        return lax.psum(shard, "rep")
    rows, width = shard.shape
    copies = lax.axis_size("rep")
    padded = -(-rows // copies) * copies
    if padded != rows:
        shard = jnp.pad(shard, ((0, padded - rows), (0, 0)))
    part = lax.psum_scatter(shard, "rep", scatter_dimension=0, tiled=True)
    return lax.all_gather(part, "rep", axis=0, tiled=True)


def local(
    tokens,
    segment,
    attn_gain,
    w_query,
    key_weight,
    value_weight,
    w_out,
    mlp_gain,
    gate_weight,
    up_weight,
    down_weight,
    cotangent,
):
    devices = lax.axis_size("fsdp")
    rows, ff = gate_weight.shape[1:]
    width = rows * devices
    kv = key_weight.shape[2]
    down_rows = down_weight.shape[1]
    layouts = [geometry(piece) for piece in blocks_of(segment)]
    layout = ([item[0] for item in layouts],) + tuple(
        jnp.concatenate([item[member] for item in layouts]) for member in range(1, 4)
    )
    active_rows = layout[1]

    all_gains = jnp.concatenate([attn_gain, mlp_gain]).reshape(1, 4 * rows)
    all_gains = jnp.pad(all_gains, ((0, 0), (0, 2 * width + 2 * kv - 4 * rows)))
    attn_weights, feed_weights = [], []
    gains = None
    for layer in range(DECODER_LAYERS):
        packed = jnp.concatenate(
            [w_query[layer], key_weight[layer], value_weight[layer], w_out[layer]], axis=1
        )
        if layer == 0:
            packed = jnp.concatenate([packed, all_gains])
        whole = lax.all_gather(packed, "fsdp", axis=0, tiled=False)
        if layer == 0:
            gains = whole[:, rows, : 4 * rows].reshape(devices, 4, rows)
            gains = gains.transpose(1, 0, 2).reshape(4, width).astype(jnp.float32)
        whole = whole[:, :rows].reshape(width, -1)
        attn_weights.append(
            (
                whole[:, :width],
                whole[:, width : width + kv],
                whole[:, width + kv : width + 2 * kv],
                whole[:, width + 2 * kv :],
            )
        )
        packed = jnp.concatenate(
            [gate_weight[layer], up_weight[layer], down_weight[layer].reshape(rows, ff)]
        )
        whole = lax.all_gather(packed, "fsdp", axis=0, tiled=False)
        feed_weights.append(
            (
                whole[:, :rows].reshape(width, ff),
                whole[:, rows : 2 * rows].reshape(width, ff),
                whole[:, 2 * rows :].reshape(ff, width),
            )
        )

    residual = tokens.astype(jnp.float32)
    saved = []
    for layer in range(DECODER_LAYERS):
        residual, kept = layer_forward(
            residual,
            attn_weights[layer],
            feed_weights[layer],
            (gains[layer], gains[DECODER_LAYERS + layer]),
            layout,
        )
        saved.append(kept)
    out_tokens = residual.astype(jnp.bfloat16)

    upstream = cotangent.astype(jnp.float32)
    shards = [None] * DECODER_LAYERS
    for layer in reversed(range(DECODER_LAYERS)):
        grad_hidden, mlp_gain_grad, feed_grads = feed_backward(
            saved[layer],
            feed_weights[layer],
            gains[DECODER_LAYERS + layer],
            active_rows,
            upstream,
        )
        buffer = jnp.concatenate(
            [
                feed_grads[0].reshape(devices, rows, ff),
                feed_grads[1].reshape(devices, rows, ff),
                feed_grads[2].reshape(devices, rows, ff),
            ],
            axis=1,
        )
        feed_shard = sum_shards(buffer, False)
        upstream, attn_gain_grad, attn_grads = attention_part_backward(
            saved[layer], attn_weights[layer], gains[layer], layout, grad_hidden
        )
        gain_grads = jnp.concatenate(
            [attn_gain_grad.reshape(devices, rows), mlp_gain_grad.reshape(devices, rows)], axis=1
        ).astype(jnp.bfloat16)
        gain_grads = jnp.pad(gain_grads, ((0, 0), (0, 2 * width + 2 * kv - 2 * rows)))
        buffer = jnp.concatenate(
            [
                jnp.concatenate(attn_grads, axis=1).reshape(devices, rows, -1),
                gain_grads[:, None],
            ],
            axis=1,
        )
        attn_shard = sum_shards(buffer, layer == 0)
        feed_shard = feed_shard.astype(jnp.float32)
        attn_shard = attn_shard.astype(jnp.float32)
        block = attn_shard[:rows]
        shards[layer] = (
            attn_shard[rows, :rows],
            block[:, :width],
            block[:, width : width + kv],
            block[:, width + kv : width + 2 * kv],
            block[:, width + 2 * kv :],
            attn_shard[rows, rows : 2 * rows],
            feed_shard[:rows],
            feed_shard[rows : 2 * rows],
            feed_shard[2 * rows : 3 * rows].reshape(down_rows, width),
        )
    stacked = tuple(
        jnp.stack([shards[layer][member] for layer in range(DECODER_LAYERS)])
        for member in range(9)
    )
    return (out_tokens, upstream) + stacked


def solution(mesh):
    in_specs = (
        P(("rep", "fsdp"), None),
        P(("rep", "fsdp")),
        P(None, "fsdp"),
        P(None, "fsdp", None),
        P(None, "fsdp", None),
        P(None, "fsdp", None),
        P(None, "fsdp", None),
        P(None, "fsdp"),
        P(None, "fsdp", None),
        P(None, "fsdp", None),
        P(None, "fsdp", None),
        P(("rep", "fsdp"), None),
    )
    out_specs = (
        P(("rep", "fsdp"), None),
        P(("rep", "fsdp"), None),
        P(None, "fsdp"),
        P(None, "fsdp", None),
        P(None, "fsdp", None),
        P(None, "fsdp", None),
        P(None, "fsdp", None),
        P(None, "fsdp"),
        P(None, "fsdp", None),
        P(None, "fsdp", None),
        P(None, "fsdp", None),
    )
    return jax.shard_map(local, mesh=mesh, in_specs=in_specs, out_specs=out_specs, check_vma=False)
```

```python
import jax
import jax.numpy as jnp
from jax import lax
from jax.experimental import pallas as pl
from jax.experimental.pallas import tpu as pltpu
from jax.sharding import PartitionSpec as P

QUERY_HEADS = 9
KEY_VALUE_HEADS = 3
HEAD_WIDTH = 64
DECODER_LAYERS = 2
MICRO = 2


epsilon = 1e-05
rope_base = 100000.0
masked_fill = -1e30


def geometry(segment):
    count_of_rows = segment.shape[-1]
    row_index = jnp.arange(count_of_rows, dtype=jnp.int32)
    same_segment = segment[..., :, None] == segment[..., None, :]
    earlier = row_index[None, :] < row_index[:, None]
    position = jnp.sum(jnp.where(same_segment & earlier, 1, 0).astype(jnp.int32), axis=-1)
    allowed = same_segment & (row_index[None, :] <= row_index[:, None])
    active_rows = jnp.where(segment >= 0, 1.0, 0.0).astype(jnp.float32)[..., None]
    frequency = rope_base ** (-2.0 * jnp.arange(HEAD_WIDTH // 2, dtype=jnp.float32) / HEAD_WIDTH)
    angles = position.astype(jnp.float32)[..., None] * frequency
    return (allowed, active_rows, jnp.cos(angles)[..., None, :], jnp.sin(angles)[..., None, :])


def rotary_apply(vectors, cosine_table, sine_values):
    half_width = vectors.shape[-1] // 2
    first_half = vectors[..., :half_width]
    second_half = vectors[..., half_width:]
    return jnp.concatenate(
        [
            first_half * cosine_table - second_half * sine_values,
            second_half * cosine_table + first_half * sine_values,
        ],
        axis=-1,
    )


def rotary_inverse(vectors, cosine_table, sine_values):
    half_width = vectors.shape[-1] // 2
    first_half = vectors[..., :half_width]
    second_half = vectors[..., half_width:]
    return jnp.concatenate(
        [
            first_half * cosine_table + second_half * sine_values,
            second_half * cosine_table - first_half * sine_values,
        ],
        axis=-1,
    )


def norm_forward(value_rows, gain_row):
    factor = lax.rsqrt(jnp.mean(value_rows * value_rows, axis=-1, keepdims=True) + epsilon)
    return (value_rows * factor * gain_row, factor)


def norm_backward(value_rows, factor, gain_row, upstream):
    scaled = upstream * gain_row
    through = factor * scaled - value_rows * (factor * factor * factor) * jnp.mean(
        scaled * value_rows, axis=-1, keepdims=True
    )
    return (through, jnp.sum(upstream * value_rows * factor, axis=0))


def row_tile(count_of_rows):
    return 256 if count_of_rows % 256 == 0 else count_of_rows


def tile_mask(column_ref, row_ref, start, size):
    reach = start + size
    shape = (size, reach)
    row_number = lax.broadcasted_iota(jnp.int32, shape, 0) + start
    key_number = lax.broadcasted_iota(jnp.int32, shape, 1)
    same = column_ref[start : start + size, :] == row_ref[0, :, :reach]
    allowed = jnp.where(same & (key_number <= row_number), 1.0, 0.0)
    return jnp.concatenate([allowed] * (QUERY_HEADS // KEY_VALUE_HEADS), axis=0) > 0.5


def head_stack(ref, start, size, group):
    heads = QUERY_HEADS // KEY_VALUE_HEADS
    first = group * heads * HEAD_WIDTH
    piece = ref[start : start + size, first : first + heads * HEAD_WIDTH]
    return jnp.concatenate(
        [piece[:, j * HEAD_WIDTH : (j + 1) * HEAD_WIDTH] for j in range(heads)], axis=0
    )


def head_unstack(stacked, size):
    heads = QUERY_HEADS // KEY_VALUE_HEADS
    return [stacked[j * size : (j + 1) * size] for j in range(heads)]


def dot_rows(left, right):
    return lax.dot_general(
        left, right, (((0,), (0,)), ((), ())), preferred_element_type=jnp.float32
    )


def forward_kernel(column_ref, row_ref, query_ref, key_ref, value_ref, mixed_ref, total_ref):
    count_of_rows = query_ref.shape[0]
    size = row_tile(count_of_rows)
    scale = HEAD_WIDTH ** (-0.5)
    for start in range(0, count_of_rows, size):
        reach = start + size
        allowed = tile_mask(column_ref, row_ref, start, size)
        outputs, totals = [], []
        for group in range(KEY_VALUE_HEADS):
            lanes = slice(group * HEAD_WIDTH, (group + 1) * HEAD_WIDTH)
            queries = head_stack(query_ref, start, size, group)
            scores = times_transposed(queries, key_ref[:reach, lanes]) * scale
            scores = jnp.where(allowed, scores, masked_fill)
            peak = jnp.max(scores, axis=-1, keepdims=True)
            expo = jnp.exp(scores - peak)
            total = jnp.sum(expo, axis=-1, keepdims=True)
            probs = (expo * (1.0 / total)).astype(jnp.bfloat16)
            mixed = jnp.dot(probs, value_ref[:reach, lanes], preferred_element_type=jnp.float32)
            outputs += head_unstack(mixed, size)
            totals += head_unstack(peak + jnp.log(total), size)
        mixed_ref[start:reach, :] = jnp.concatenate(outputs, axis=1).astype(jnp.bfloat16)
        total_ref[start:reach, :] = jnp.concatenate(totals, axis=1)


def backward_kernel(
    column_ref,
    row_ref,
    query_ref,
    key_ref,
    value_ref,
    total_ref,
    upstream_ref,
    grad_query_ref,
    grad_key_ref,
    grad_value_ref,
):
    count_of_rows = query_ref.shape[0]
    size = row_tile(count_of_rows)
    scale = HEAD_WIDTH ** (-0.5)
    heads = QUERY_HEADS // KEY_VALUE_HEADS
    for start in reversed(range(0, count_of_rows, size)):
        reach = start + size
        allowed = tile_mask(column_ref, row_ref, start, size)
        query_grads, key_grads, value_grads = [], [], []
        for group in range(KEY_VALUE_HEADS):
            lanes = slice(group * HEAD_WIDTH, (group + 1) * HEAD_WIDTH)
            queries = head_stack(query_ref, start, size, group)
            upstream = head_stack(upstream_ref, start, size, group)
            keys = key_ref[:reach, lanes]
            values = value_ref[:reach, lanes]
            totals = total_ref[start:reach, :]
            total = jnp.concatenate(
                [totals[:, group * heads + j : group * heads + j + 1] for j in range(heads)], axis=0
            )
            scores = times_transposed(queries, keys) * scale
            scores = jnp.where(allowed, scores, masked_fill)
            probs_full = jnp.exp(scores - total)
            value_grads.append(dot_rows(probs_full.astype(jnp.bfloat16), upstream))
            grad_probs = times_transposed(upstream, values)
            row_weight = jnp.sum(probs_full * grad_probs, axis=-1, keepdims=True)
            grad_scores = (probs_full * (grad_probs - row_weight)).astype(jnp.bfloat16)
            grad_queries = jnp.dot(grad_scores, keys, preferred_element_type=jnp.float32) * scale
            query_grads += head_unstack(grad_queries, size)
            key_grads.append(dot_rows(grad_scores, queries) * scale)
        grad_query_ref[start:reach, :] = jnp.concatenate(query_grads, axis=1)
        key_grads = jnp.concatenate(key_grads, axis=1)
        value_grads = jnp.concatenate(value_grads, axis=1)
        if reach == count_of_rows:
            grad_key_ref[...] = key_grads
            grad_value_ref[...] = value_grads
        else:
            grad_key_ref[:reach, :] += key_grads
            grad_value_ref[:reach, :] += value_grads


def row_spec(size, width):
    return pl.BlockSpec((size, width), lambda index: (index, 0))


def call_attention(kernel, segment, arrays, outputs):
    size = segment.shape[0] // MICRO
    return pl.pallas_call(
        kernel,
        grid=(MICRO,),
        in_specs=[row_spec(size, 1), pl.BlockSpec((1, 1, size), lambda index: (index, 0, 0))]
        + [row_spec(size, item.shape[1]) for item in arrays],
        out_specs=[row_spec(size, item.shape[1]) for item in outputs],
        out_shape=outputs,
        compiler_params=pltpu.CompilerParams(vmem_limit_bytes=50 * 2**20),
    )(segment.reshape(-1, 1), segment.reshape(MICRO, 1, size), *arrays)


def attend(query_rows, key_rows, value_rows, segment):
    count_of_rows = query_rows.shape[0]
    return call_attention(
        forward_kernel,
        segment,
        (query_rows, key_rows, value_rows),
        [
            jax.ShapeDtypeStruct(query_rows.shape, jnp.bfloat16),
            jax.ShapeDtypeStruct((count_of_rows, QUERY_HEADS), jnp.float32),
        ],
    )


def attend_back(query_rows, key_rows, value_rows, log_total, mixed_gradient, segment):
    return call_attention(
        backward_kernel,
        segment,
        (query_rows, key_rows, value_rows, log_total, mixed_gradient),
        [
            jax.ShapeDtypeStruct(item.shape, jnp.float32)
            for item in (query_rows, key_rows, value_rows)
        ],
    )


def rotate_flat(rotation, rows, cosine_table, sine_values):
    shaped = rows.reshape(rows.shape[0], -1, HEAD_WIDTH)
    return rotation(shaped, cosine_table, sine_values).reshape(rows.shape).astype(jnp.bfloat16)


def layer_forward(residual, attn_params, fetch_feed, gains, layout):
    allowed, active_rows, cosine_table, sine_values = layout
    w_query, key_weight, value_weight, w_out = attn_params
    normed, factor = norm_forward(residual, gains[0])
    normed = normed.astype(jnp.bfloat16)
    query_rows = jnp.dot(normed, w_query, preferred_element_type=jnp.float32)
    key_rows = jnp.dot(normed, key_weight, preferred_element_type=jnp.float32)
    value_rows = jnp.dot(normed, value_weight, preferred_element_type=jnp.float32).astype(
        jnp.bfloat16
    )
    query_rows = rotate_flat(rotary_apply, query_rows, cosine_table, sine_values)
    key_rows = rotate_flat(rotary_apply, key_rows, cosine_table, sine_values)
    mixed, log_total = attend(query_rows, key_rows, value_rows, allowed)
    hidden_state = (
        residual + jnp.dot(mixed, w_out, preferred_element_type=jnp.float32) * active_rows
    )
    gate_weight, up_weight, down_weight = fetch_feed
    normed_feed, factor_mlp = norm_forward(hidden_state, gains[1])
    normed_feed = normed_feed.astype(jnp.bfloat16)
    gate_branch = jnp.dot(normed_feed, gate_weight, preferred_element_type=jnp.float32)
    up_branch = jnp.dot(normed_feed, up_weight, preferred_element_type=jnp.float32)
    inner_product = (jax.nn.silu(gate_branch) * up_branch).astype(jnp.bfloat16)
    output = (
        hidden_state
        + jnp.dot(inner_product, down_weight, preferred_element_type=jnp.float32) * active_rows
    )
    saved = (
        residual,
        normed,
        factor,
        query_rows,
        key_rows,
        value_rows,
        mixed,
        log_total,
        hidden_state,
        normed_feed,
        factor_mlp,
        gate_branch,
        up_branch,
        inner_product,
    )
    return (output, saved)


def contract_rows(left, right):
    return lax.dot_general(
        left, right, (((0,), (0,)), ((), ())), preferred_element_type=jnp.float32
    ).astype(jnp.bfloat16)


def times_transposed(left, right):
    return lax.dot_general(
        left, right, (((1,), (1,)), ((), ())), preferred_element_type=jnp.float32
    )


def feed_backward(saved, feed_params, gain_row, active_rows, upstream):
    hidden_state, normed_feed, factor_mlp, gate_branch, up_branch, inner_product = saved[8:]
    gate_weight, up_weight, down_weight = feed_params
    sigmoid_gate = jax.nn.sigmoid(gate_branch)
    activated = gate_branch * sigmoid_gate
    grad_branch = (upstream * active_rows).astype(jnp.bfloat16)
    grad_inner = times_transposed(grad_branch, down_weight).astype(jnp.bfloat16)
    grad_gate_in = (
        grad_inner * up_branch * sigmoid_gate * (1.0 + gate_branch * (1.0 - sigmoid_gate))
    ).astype(jnp.bfloat16)
    grad_up_in = (grad_inner * activated).astype(jnp.bfloat16)
    grad_down = contract_rows(inner_product, grad_branch)
    grad_gate = contract_rows(normed_feed, grad_gate_in)
    grad_up = contract_rows(normed_feed, grad_up_in)
    grad_normed = times_transposed(grad_gate_in, gate_weight) + times_transposed(
        grad_up_in, up_weight
    )
    through, grad_gain = norm_backward(hidden_state, factor_mlp, gain_row, grad_normed)
    return (through + upstream, grad_gain, (grad_gate, grad_up, grad_down))


def attention_part_backward(saved, attn_params, gain_row, layout, grad_hidden):
    residual, normed, factor, query_rows, key_rows, value_rows, mixed, log_total = saved[:8]
    w_query, key_weight, value_weight, w_out = attn_params
    allowed, active_rows, cosine_table, sine_values = layout
    grad_attn = (grad_hidden * active_rows).astype(jnp.bfloat16)
    grad_out = contract_rows(mixed, grad_attn)
    mixed_gradient = times_transposed(grad_attn, w_out).astype(jnp.bfloat16)
    grad_queries, key_gradient, value_gradient = attend_back(
        query_rows, key_rows, value_rows, log_total, mixed_gradient, allowed
    )
    value_gradient = value_gradient.astype(jnp.bfloat16)
    grad_queries = rotate_flat(rotary_inverse, grad_queries, cosine_table, sine_values)
    key_gradient = rotate_flat(rotary_inverse, key_gradient, cosine_table, sine_values)
    grad_query = contract_rows(normed, grad_queries)
    grad_key = contract_rows(normed, key_gradient)
    grad_value = contract_rows(normed, value_gradient)
    grad_normed = (
        times_transposed(grad_queries, w_query)
        + times_transposed(key_gradient, key_weight)
        + times_transposed(value_gradient, value_weight)
    )
    through, grad_gain = norm_backward(residual, factor, gain_row, grad_normed)
    return (through + grad_hidden, grad_gain, (grad_query, grad_key, grad_value, grad_out))


def blocks_of(rows):
    size = rows.shape[0] // MICRO
    return [rows[index * size : (index + 1) * size] for index in range(MICRO)]


def sum_shards(buffer, last):
    shard = lax.psum_scatter(buffer, "fsdp", scatter_dimension=0, tiled=False)
    if last:
        return lax.psum(shard, "rep")
    rows, width = shard.shape
    copies = lax.axis_size("rep")
    padded = -(-rows // copies) * copies
    if padded != rows:
        shard = jnp.pad(shard, ((0, padded - rows), (0, 0)))
    part = lax.psum_scatter(shard, "rep", scatter_dimension=0, tiled=True)
    return lax.all_gather(part, "rep", axis=0, tiled=True)


def local(
    tokens,
    segment,
    attn_gain,
    w_query,
    key_weight,
    value_weight,
    w_out,
    mlp_gain,
    gate_weight,
    up_weight,
    down_weight,
    cotangent,
):
    devices = lax.axis_size("fsdp")
    rows, ff = gate_weight.shape[1:]
    width = rows * devices
    kv = key_weight.shape[2]
    down_rows = down_weight.shape[1]
    layouts = [geometry(piece) for piece in blocks_of(segment)]
    layout = (segment,) + tuple(
        jnp.concatenate([item[member] for item in layouts]) for member in range(1, 4)
    )
    active_rows = layout[1]

    all_gains = jnp.concatenate([attn_gain, mlp_gain]).reshape(1, 4 * rows)
    all_gains = jnp.pad(all_gains, ((0, 0), (0, 2 * width + 2 * kv - 4 * rows)))
    attn_weights, feed_weights = [], []
    gains = None
    for layer in range(DECODER_LAYERS):
        packed = jnp.concatenate(
            [w_query[layer], key_weight[layer], value_weight[layer], w_out[layer]], axis=1
        )
        if layer == 0:
            packed = jnp.concatenate([packed, all_gains])
        whole = lax.all_gather(packed, "fsdp", axis=0, tiled=False)
        if layer == 0:
            gains = whole[:, rows, : 4 * rows].reshape(devices, 4, rows)
            gains = gains.transpose(1, 0, 2).reshape(4, width).astype(jnp.float32)
        whole = whole[:, :rows].reshape(width, -1)
        attn_weights.append(
            (
                whole[:, :width],
                whole[:, width : width + kv],
                whole[:, width + kv : width + 2 * kv],
                whole[:, width + 2 * kv :],
            )
        )
        packed = jnp.concatenate(
            [gate_weight[layer], up_weight[layer], down_weight[layer].reshape(rows, ff)]
        )
        whole = lax.all_gather(packed, "fsdp", axis=0, tiled=False)
        feed_weights.append(
            (
                whole[:, :rows].reshape(width, ff),
                whole[:, rows : 2 * rows].reshape(width, ff),
                whole[:, 2 * rows :].reshape(ff, width),
            )
        )

    residual = tokens.astype(jnp.float32)
    saved = []
    for layer in range(DECODER_LAYERS):
        residual, kept = layer_forward(
            residual,
            attn_weights[layer],
            feed_weights[layer],
            (gains[layer], gains[DECODER_LAYERS + layer]),
            layout,
        )
        saved.append(kept)
    out_tokens = residual.astype(jnp.bfloat16)

    upstream = cotangent.astype(jnp.float32)
    shards = [None] * DECODER_LAYERS
    for layer in reversed(range(DECODER_LAYERS)):
        grad_hidden, mlp_gain_grad, feed_grads = feed_backward(
            saved[layer],
            feed_weights[layer],
            gains[DECODER_LAYERS + layer],
            active_rows,
            upstream,
        )
        buffer = jnp.concatenate(
            [
                feed_grads[0].reshape(devices, rows, ff),
                feed_grads[1].reshape(devices, rows, ff),
                feed_grads[2].reshape(devices, rows, ff),
            ],
            axis=1,
        )
        feed_shard = sum_shards(buffer, False)
        upstream, attn_gain_grad, attn_grads = attention_part_backward(
            saved[layer], attn_weights[layer], gains[layer], layout, grad_hidden
        )
        gain_grads = jnp.concatenate(
            [attn_gain_grad.reshape(devices, rows), mlp_gain_grad.reshape(devices, rows)], axis=1
        ).astype(jnp.bfloat16)
        gain_grads = jnp.pad(gain_grads, ((0, 0), (0, 2 * width + 2 * kv - 2 * rows)))
        buffer = jnp.concatenate(
            [
                jnp.concatenate(attn_grads, axis=1).reshape(devices, rows, -1),
                gain_grads[:, None],
            ],
            axis=1,
        )
        attn_shard = sum_shards(buffer, layer == 0)
        feed_shard = feed_shard.astype(jnp.float32)
        attn_shard = attn_shard.astype(jnp.float32)
        block = attn_shard[:rows]
        shards[layer] = (
            attn_shard[rows, :rows],
            block[:, :width],
            block[:, width : width + kv],
            block[:, width + kv : width + 2 * kv],
            block[:, width + 2 * kv :],
            attn_shard[rows, rows : 2 * rows],
            feed_shard[:rows],
            feed_shard[rows : 2 * rows],
            feed_shard[2 * rows : 3 * rows].reshape(down_rows, width),
        )
    stacked = tuple(
        jnp.stack([shards[layer][member] for layer in range(DECODER_LAYERS)])
        for member in range(9)
    )
    return (out_tokens, upstream) + stacked


def solution(mesh):
    in_specs = (
        P(("rep", "fsdp"), None),
        P(("rep", "fsdp")),
        P(None, "fsdp"),
        P(None, "fsdp", None),
        P(None, "fsdp", None),
        P(None, "fsdp", None),
        P(None, "fsdp", None),
        P(None, "fsdp"),
        P(None, "fsdp", None),
        P(None, "fsdp", None),
        P(None, "fsdp", None),
        P(("rep", "fsdp"), None),
    )
    out_specs = (
        P(("rep", "fsdp"), None),
        P(("rep", "fsdp"), None),
        P(None, "fsdp"),
        P(None, "fsdp", None),
        P(None, "fsdp", None),
        P(None, "fsdp", None),
        P(None, "fsdp", None),
        P(None, "fsdp"),
        P(None, "fsdp", None),
        P(None, "fsdp", None),
        P(None, "fsdp", None),
    )
    return jax.shard_map(local, mesh=mesh, in_specs=in_specs, out_specs=out_specs, check_vma=False)
```
